1024 devices in a mesh: gx: 32 (over x, z_lo), gy: 32 (over z_hi, y, core).
Axes of the slice: x: 8, y: 8, z: 8 (z_hi: 2, z_lo: 4; z = z_hi * 4 + z_lo), core: 2. Of those that a mesh axis runs over, the one named last changes fastest.
Arguments:
- composition: float32 [53, 1024, 4096], P(None, 'gx', 'gy'), may hold values from -6 to 6
- inverse_temp: float32 [1024, 4096], P('gx', 'gy'), may hold values from 0.3 to 1.2
- sections: int32 [1024, 32], P('gx', 'gy'), may hold values from 2 to 12, as said below
- reactant_orders: float32 [325, 53], replicated, may hold values from -0.875 to 0.875
- net_stoich: float32 [53, 325], replicated, may hold values from -0.3125 to 0.3125
- log_prefactor: float32 [325], replicated, may hold values from -1 to 1
- activation: float32 [325], replicated, may hold values from 0.5 to 3
- diffusivity: float32 [53], replicated, may hold values from 0.04 to 0.2
Outputs:
- state_next: float32 [53, 1024, 4096], P(None, 'gx', 'gy')
The draws below stay inside these ranges and needn't reach their ends.
Inputs may be any that keep to these rules, and one draw needn't show every extreme that they name: Every draw has blocks with 12 sections and blocks with 2 sections.
All inputs are finite; a program needn't handle non-finite values.
Results may differ from the reference program's by a relative error of at most 0.0003.
Values sent between devices are 32-bit elements; how exact they have to be, the bound alone decides.
A program may use at most 32 MiB of HBM per device.

```python
import math
import jax
import jax.numpy as jnp
from jax import lax

S = 53
R = 325
BLOCK = 128
MOST_SECTIONS = 12
FEWEST_SECTIONS = 2
NX = 1024
NY = 4096
N_GY = 32


def draw_sections(key, part):
    key = jax.random.fold_in(key, 11)
    key_front, key_jitter = jax.random.split(key, 2)
    front_rows = jax.random.randint(key_front, (N_GY,), 0, NX)
    row_index = jnp.arange(NX)[:, None]
    distance = jnp.abs(row_index - front_rows[None, :])
    distance = jnp.minimum(distance, NX - distance)
    band_rows = max(NX // 16, 1)
    profile = MOST_SECTIONS - 10 * distance // band_rows
    jitter = jax.random.randint(key_jitter, (NX, N_GY), 0, 3)
    counts = jnp.clip(profile + jitter, FEWEST_SECTIONS, MOST_SECTIONS)
    counts = jnp.where(distance == 0, MOST_SECTIONS, counts)
    counts = jnp.where(distance == NX // 2, FEWEST_SECTIONS, counts)
    return counts.astype(jnp.int32)


def level_of(key, dims, cuts, low, top_value):
    def one(axis_at, parts):
        steps = jax.random.uniform(jax.random.fold_in(jax.random.fold_in(key, 6), axis_at), (parts,), jnp.float32, low / len(cuts), top_value / len(cuts))
        return jnp.repeat(jnp.exp(steps), dims[axis_at] // parts).reshape((-1,) + (1,) * (len(dims) - axis_at - 1))

    level = one(*cuts[0])
    for cut in cuts[1:]:
        level = level * one(*cut)
    return level


def bell_draw(key, dims, deviation, reach, cuts=(), dtype=jnp.bfloat16):
    result = deviation * jax.random.normal(key, dims, jnp.float32)
    if cuts:
        result = result * level_of(key, dims, cuts, -0.22, 0.18)
    return jnp.clip(result, -reach, reach).astype(dtype)


def setup_inputs(seed: int = 0) -> dict:
    arg_keys = jax.random.split(jax.random.key(seed), 9)
    composition = bell_draw(arg_keys[0], (S, NX, NY), 1.0, 6.0, ((1, 32), (2, 32)), jnp.float32)
    inverse_temp = jnp.clip(0.3 + 0.90000004 * jax.random.uniform(arg_keys[1], (NX, NY), jnp.float32) ** level_of(arg_keys[1], (NX, NY), ((0, 32), (1, 32)), -0.2, 0.2), 0.3, 1.2)
    sections = draw_sections(jax.random.fold_in(arg_keys[8], 71), 0)
    reactant_orders = bell_draw(arg_keys[3], (R, S), S ** -0.5, 0.875, (), jnp.float32)
    net_stoich = bell_draw(arg_keys[4], (S, R), R ** -0.5, 0.3125, (), jnp.float32)
    log_prefactor = jnp.clip(jax.random.uniform(arg_keys[5], (R,), jnp.float32, -1.0, 1.0), -1.0, 1.0)
    activation = jnp.clip(jnp.exp(jax.random.uniform(arg_keys[6], (R,), jnp.float32, math.log(0.5), math.log(3.0))), 0.5, 3.0)
    diffusivity = jnp.clip(jnp.exp(jax.random.uniform(arg_keys[7], (S,), jnp.float32, math.log(0.04), math.log(0.2))), 0.04, 0.2)
    return dict(composition=composition, inverse_temp=inverse_temp, sections=sections, reactant_orders=reactant_orders, net_stoich=net_stoich, log_prefactor=log_prefactor, activation=activation, diffusivity=diffusivity)


spectrum_mid = 4.5
spectrum_half = 3.5


def relax_group(start_state, theta_cells, counts_group, reactant_orders, net_stoich, log_prefactor, activation):
    rate_cells = jnp.exp(log_prefactor[:, None] - activation[:, None] * theta_cells[None, :])
    cells_each = theta_cells.shape[0] // counts_group.shape[0]
    count_float = counts_group.astype(jnp.float32)

    def section(section_idx, current):
        cheb_node = jnp.cos(jnp.pi * (2 * section_idx + 1).astype(jnp.float32) / (2.0 * count_float))
        step_size = 1.0 / (spectrum_mid + spectrum_half * cheb_node)
        step_size = jnp.where(section_idx < counts_group, step_size, 0.0)
        step_cells = jnp.repeat(step_size, cells_each)
        drive = jnp.dot(reactant_orders, current, precision=lax.Precision.HIGHEST)
        forward = rate_cells * jax.nn.sigmoid(drive)
        source = jnp.dot(net_stoich, forward, precision=lax.Precision.HIGHEST)
        return current - step_cells[None, :] * (current - start_state - source)

    return lax.fori_loop(0, jnp.max(counts_group), section, start_state)


def chem_blocks(block_state, block_temps, counts, reactant_orders, net_stoich, log_prefactor, activation, group):
    species, block_count, cells = block_state.shape
    group_count = block_count // group
    block_order = jnp.argsort(-counts, stable=True)
    group_state = jnp.moveaxis(block_state[:, block_order].reshape(species, group_count, group * cells), 1, 0)
    group_temps = block_temps[block_order].reshape(group_count, group * cells)
    group_counts = counts[block_order].reshape(group_count, group)

    def run_group(group_item):
        return relax_group(group_item[0], group_item[1], group_item[2], reactant_orders, net_stoich, log_prefactor, activation)

    relaxed = lax.map(run_group, (group_state, group_temps, group_counts))
    relaxed = jnp.moveaxis(relaxed, 0, 1).reshape(species, block_count, cells)
    inverse_order = jnp.argsort(block_order)
    return relaxed[:, inverse_order]


def reference(composition, inverse_temp, sections, reactant_orders, net_stoich, log_prefactor, activation, diffusivity):
    block_state = composition.reshape(S, NX * N_GY, BLOCK)
    block_temps = inverse_temp.reshape(NX * N_GY, BLOCK)
    counts = sections.reshape(NX * N_GY).astype(jnp.int32)
    reacted = chem_blocks(block_state, block_temps, counts, reactant_orders, net_stoich, log_prefactor, activation, 32)
    state_field = reacted.reshape(S, NX, NY)
    padded = jnp.pad(state_field, ((0, 0), (1, 1), (1, 1)))
    laplace_term = padded[:, 2:, 1:-1] + padded[:, :-2, 1:-1] + padded[:, 1:-1, 2:] + padded[:, 1:-1, :-2] - 4.0 * state_field
    return state_field + diffusivity[:, None, None] * laplace_term
```

```python
import functools

import jax
import jax.numpy as jnp
import numpy as np
from jax import lax
from jax.experimental import pallas as pl
from jax.experimental.pallas import tpu as pltpu
from jax.sharding import PartitionSpec as P

SPECIES = 53
REACTIONS = 325
ROWS = 32
CELLS = 128
MOST = 12
S_PAD = 56
V_PAD = 64
R_PAD = 352
WIDE = ROWS * CELLS
CHUNKS = ROWS // 2
F8_SECTIONS = 9
BF_SECTIONS = 2
UNROLL = 3
LAG = 8
PAIR = 4
ORDER_SCALE = 8.0
STOICH_SCALE = 64.0
RATE_SCALE = 32.0

bf16 = jnp.bfloat16
f8 = jnp.float8_e4m3fn
f32 = jnp.float32
MESH = pl.DeviceIdType.MESH


def step_table():
    table = np.zeros((16, MOST), np.float32)
    for count in range(1, MOST + 1):
        for j in range(count):
            node = np.cos(np.pi * (2 * j + 1) / (2 * count))
            table[count, MOST - count + j] = 1.0 / (4.5 + 3.5 * node)
    return table


def split(value, dtype):
    high = value.astype(dtype)
    return high, (value - high.astype(f32)).astype(dtype)


def dot(left, right):
    return jnp.dot(left, right, preferred_element_type=f32)


def block(b):
    return pl.ds(b * CELLS, CELLS)


def chunk(c):
    return pl.ds(c * 2 * CELLS, 2 * CELLS)


def kernel(
    sec_hbm, tab_hbm, comp_hbm, theta_hbm, orders_hbm, stoich_hbm, prefactor_hbm, activation_hbm,
    diff_hbm, out, sec, tab, comp, theta, orders, stoich, log_prefactor, activation, diffusivity, vs, base, rate, rate_b, f_b, f_8, orders_8, orders_b, stoich_8, stoich_b,
    prefactor_col, activation_col, diff_col, edges, halo, load_sems, send_sems, recv_sems,
):
    gx, gy = lax.axis_index("gx"), lax.axis_index("gy")
    nx, ny = lax.axis_size("gx"), lax.axis_size("gy")
    sides = (
        (gx > 0, (gx - 1, gy)),
        (gx < nx - 1, (gx + 1, gy)),
        (gy > 0, (gx, gy - 1)),
        (gy < ny - 1, (gx, gy + 1)),
    )
    peers = (gx + nx - 1) // nx + (2 * nx - 2 - gx) // nx
    peers = peers + (gy + ny - 1) // ny + (2 * ny - 2 - gy) // ny
    pairs = (
        (theta_hbm, theta),
        (prefactor_hbm, log_prefactor),
        (activation_hbm, activation),
        (stoich_hbm, stoich),
        (orders_hbm, orders),
        (diff_hbm, diffusivity),
        (sec_hbm, sec),
        (tab_hbm, tab),
        (comp_hbm, comp),
    )
    loads = [pltpu.make_async_copy(a, b, load_sems.at[i]) for i, (a, b) in enumerate(pairs)]
    for load in loads:
        load.start()
    barrier = pltpu.get_barrier_semaphore()
    for there, device in sides:

        @pl.when(there)
        def _(device=device):
            pl.semaphore_signal(barrier, inc=1, device_id=device, device_id_type=MESH)

    for k, (there, _) in enumerate(sides):

        @pl.when(jnp.logical_not(there))
        def _(k=k):
            halo[k] = jnp.zeros((S_PAD, CELLS), f32)

    for load in loads[:-1]:
        load.wait()
    orders_f = jnp.concatenate([orders[...] * 0.5, jnp.zeros((V_PAD - SPECIES, REACTIONS), f32)], 0)
    orders_f = jnp.concatenate([orders_f, jnp.zeros((V_PAD, 384 - REACTIONS), f32)], 1)
    orders_f = jnp.transpose(orders_f)[:R_PAD]
    high, low = split(orders_f, bf16)
    orders_b[...] = jnp.concatenate([high, high, low], 1)
    high, low = split(orders_f * ORDER_SCALE, f8)
    orders_8[...] = jnp.concatenate([high, high, low, low], 1)
    stoich_f = jnp.concatenate([stoich[...] * 0.5, jnp.zeros((V_PAD - SPECIES, REACTIONS), f32)], 0)
    stoich_f = jnp.concatenate([stoich_f, jnp.zeros((V_PAD, R_PAD - REACTIONS), f32)], 1)
    high, low = split(stoich_f * (1.0 / RATE_SCALE), bf16)
    stoich_b[...] = jnp.concatenate([high, low], 0)
    stoich_8[...] = (stoich_f * STOICH_SCALE).astype(f8)
    rows = [log_prefactor[...].reshape(1, REACTIONS), activation[...].reshape(1, REACTIONS)]
    rows = jnp.concatenate(rows + [jnp.zeros((6, REACTIONS), f32)], 0)
    rows = jnp.concatenate([rows, jnp.zeros((8, 384 - REACTIONS), f32)], 1)
    columns = jnp.transpose(rows)
    prefactor_col[...] = jnp.broadcast_to(columns[:R_PAD, 0:1], (R_PAD, CELLS))
    activation_col[...] = jnp.broadcast_to(columns[:R_PAD, 1:2], (R_PAD, CELLS))
    rows = jnp.concatenate([diffusivity[...], jnp.zeros((1, CELLS - SPECIES), f32)], 1)
    rows = jnp.concatenate([rows, jnp.zeros((7, CELLS), f32)], 0)
    diff_col[...] = jnp.broadcast_to(jnp.transpose(rows)[:S_PAD, 0:1], (S_PAD, CELLS))

    for b in range(ROWS):
        r = jnp.exp(prefactor_col[...] - activation_col[...] * theta[b : b + 1, :]) * RATE_SCALE
        rate[:, block(b)] = r
        rate_b[:, block(b)] = r.astype(bf16)

    loads[-1].wait()

    def start_of(b):
        value = comp[pl.ds(b, SPECIES, stride=ROWS), :]
        return jnp.concatenate([value, jnp.zeros((S_PAD - SPECIES, CELLS), f32)], 0)

    vs[S_PAD:, :] = jnp.zeros((V_PAD - S_PAD, WIDE), f32)
    for c in range(CHUNKS):
        for b in (2 * c, 2 * c + 1):
            vs[0:S_PAD, block(b)] = start_of(b)
        bias = dot(stoich_b[0:S_PAD, :], rate_b[:, chunk(c)])
        base[:, chunk(c)] = vs[0:S_PAD, chunk(c)] + bias

    def forward_f8(c):
        high, low = split(vs[:, chunk(c)] * (1.0 / ORDER_SCALE), f8)
        drive = dot(orders_8[...], jnp.concatenate([high, low, high, low], 0))
        f_8[:, chunk(c)] = (jnp.tanh(drive.astype(bf16)) * rate_b[:, chunk(c)]).astype(f8)

    def forward_bf(c):
        drive = dot(orders_b[:, 0:V_PAD], vs[:, chunk(c)].astype(bf16))
        f_b[:, chunk(c)] = (jnp.tanh(drive) * rate[:, chunk(c)]).astype(bf16)

    def update(c, j, target):
        for h in range(2):
            b = 2 * c + h
            step = tab[sec[0, b], j]
            v = vs[0:S_PAD, block(b)]
            vs[0:S_PAD, block(b)] = v + step * (target[:, h * CELLS : (h + 1) * CELLS] - v)

    def relax_f8(c, j):
        product = dot(stoich_8[...], f_8[:, chunk(c)])[0:S_PAD]
        update(c, j, base[:, chunk(c)] + product * (1.0 / (STOICH_SCALE * RATE_SCALE)))

    def relax_bf(c, j):
        update(c, j, base[:, chunk(c)] + dot(stoich_b[0:S_PAD, :], f_b[:, chunk(c)]))

    def section(j, forward, relax):
        for first in range(0, CHUNKS + LAG, PAIR):
            for c in range(first, first + PAIR):
                if c < CHUNKS:
                    forward(c)
            for c in range(first, first + PAIR):
                if LAG <= c:
                    relax(c - LAG, j)

    def sections_f8(i, _):
        for u in range(UNROLL):
            section(i * UNROLL + u, forward_f8, relax_f8)
        return 0

    lax.fori_loop(0, F8_SECTIONS // UNROLL, sections_f8, 0)
    for j in range(F8_SECTIONS, F8_SECTIONS + BF_SECTIONS):
        section(j, forward_bf, relax_bf)

    def last_section(c):
        high, low = split(vs[:, chunk(c)], bf16)
        drive = dot(orders_b[...], jnp.concatenate([high, low, high], 0))
        r = rate[:, chunk(c)]
        high, low = split(r + r * jnp.tanh(drive), bf16)
        product = dot(stoich_b[...], high)
        source = product[0:S_PAD] + product[V_PAD : V_PAD + S_PAD] + dot(stoich_b[0:S_PAD, :], low)
        start = jnp.concatenate([start_of(2 * c), start_of(2 * c + 1)], 1)
        update(c, MOST - 1, start + source)

    def send(k, source):
        return pltpu.make_async_remote_copy(
            src_ref=source,
            dst_ref=halo.at[k ^ 1],
            send_sem=send_sems.at[k],
            recv_sem=recv_sems.at[k],
            device_id=sides[k][1],
            device_id_type=MESH,
        )

    copies = [
        send(0, vs.at[0:S_PAD, block(0)]),
        send(1, vs.at[0:S_PAD, block(ROWS - 1)]),
        send(2, edges),
        send(3, edges),
    ]

    last_section(0)
    last_section(CHUNKS - 1)
    pl.semaphore_wait(barrier, peers)
    for k in (0, 1):

        @pl.when(sides[k][0])
        def _(k=k):
            copies[k].start()

    for c in range(1, CHUNKS - 1):
        last_section(c)

    lane = lax.broadcasted_iota(jnp.int32, (S_PAD, CELLS), 1)
    packed = jnp.zeros((S_PAD, CELLS), f32)
    for b in range(ROWS):
        v = vs[0:S_PAD, block(b)]
        packed = jnp.where(lane == b, pltpu.roll(v, b, 1), packed)
        packed = jnp.where(lane == 64 + b, pltpu.roll(v, (64 + b + 1) % CELLS, 1), packed)
    edges[...] = packed
    for k in (2, 3):

        @pl.when(sides[k][0])
        def _(k=k):
            copies[k].start()

    d = diff_col[...]
    for b in range(ROWS):
        v = vs[0:S_PAD, block(b)]
        total = jnp.where(lane == 0, 0.0, pltpu.roll(v, 1, 1)) - 4.0 * v
        total = total + jnp.where(lane == CELLS - 1, 0.0, pltpu.roll(v, CELLS - 1, 1))
        if b > 0:
            total = total + vs[0:S_PAD, block(b - 1)]
        if b < ROWS - 1:
            total = total + vs[0:S_PAD, block(b + 1)]
        base[:, block(b)] = v + d * total

    for k, (there, _) in enumerate(sides):

        @pl.when(there)
        def _(k=k):
            copies[k].wait_send()
            copies[k ^ 1].wait_recv()

    before, after = halo[2], halo[3]
    for b in range(ROWS):
        total = jnp.where(lane == 0, pltpu.roll(before, (CELLS - 64 - b) % CELLS, 1), 0.0)
        total = total + jnp.where(lane == CELLS - 1, pltpu.roll(after, CELLS - 1 - b, 1), 0.0)
        if b == 0:
            total = total + halo[0]
        if b == ROWS - 1:
            total = total + halo[1]
        result = base[:, block(b)] + d * total
        out[pl.ds(b, SPECIES, stride=ROWS), :] = result[0:SPECIES]


def body(
    composition,
    inverse_temp,
    sections,
    reactant_orders,
    net_stoich,
    log_prefactor,
    activation,
    diffusivity,
):
    scratch = pltpu.VMEM
    operands = (
        sections.reshape(1, ROWS),
        jnp.asarray(step_table()),
        composition.reshape(SPECIES * ROWS, CELLS),
        inverse_temp,
        reactant_orders.T,
        net_stoich,
        log_prefactor,
        activation,
        diffusivity.reshape(1, SPECIES),
    )
    operands = [pltpu.with_memory_space_constraint(x, pltpu.HBM) for x in operands]
    result = pl.pallas_call(
        kernel,
        out_shape=scratch((SPECIES * ROWS, CELLS), f32),
        in_specs=[pl.BlockSpec(memory_space=pltpu.HBM)] * 9,
        out_specs=pl.BlockSpec(memory_space=pltpu.VMEM),
        scratch_shapes=[
            pltpu.SMEM((1, ROWS), jnp.int32),
            pltpu.SMEM((16, MOST), f32),
            scratch((SPECIES * ROWS, CELLS), f32),
            scratch((ROWS, CELLS), f32),
            scratch((SPECIES, REACTIONS), f32),
            scratch((SPECIES, REACTIONS), f32),
            scratch((REACTIONS,), f32),
            scratch((REACTIONS,), f32),
            scratch((1, SPECIES), f32),
            scratch((V_PAD, WIDE), f32),
            scratch((S_PAD, WIDE), f32),
            scratch((R_PAD, WIDE), f32),
            scratch((R_PAD, WIDE), bf16),
            scratch((R_PAD, WIDE), bf16),
            scratch((R_PAD, WIDE), f8),
            scratch((R_PAD, 4 * V_PAD), f8),
            scratch((R_PAD, 3 * V_PAD), bf16),
            scratch((V_PAD, R_PAD), f8),
            scratch((2 * V_PAD, R_PAD), bf16),
            scratch((R_PAD, CELLS), f32),
            scratch((R_PAD, CELLS), f32),
            scratch((S_PAD, CELLS), f32),
            scratch((S_PAD, CELLS), f32),
            scratch((4, S_PAD, CELLS), f32),
            pltpu.SemaphoreType.DMA((9,)),
            pltpu.SemaphoreType.DMA((4,)),
            pltpu.SemaphoreType.DMA((4,)),
        ],
        compiler_params=pltpu.CompilerParams(
            collective_id=0, has_side_effects=True, vmem_limit_bytes=48 << 20
        ),
    )(*operands)
    return result.reshape(SPECIES, ROWS, CELLS)


def solution(mesh):
    return jax.shard_map(
        body,
        mesh=mesh,
        in_specs=(P(None, "gx", "gy"), P("gx", "gy"), P("gx", "gy"), P(), P(), P(), P(), P()),
        out_specs=P(None, "gx", "gy"),
        check_vma=False,
    )
```

```python
import functools

import jax
import jax.numpy as jnp
import numpy as np
from jax import lax
from jax.experimental import pallas as pl
from jax.experimental.pallas import tpu as pltpu
from jax.sharding import PartitionSpec as P

SPECIES = 53
REACTIONS = 325
ROWS = 32
CELLS = 128
MOST = 12
S_PAD = 56
V_PAD = 64
R_PAD = 352
HALO = 3
WIDE = (ROWS + HALO) * CELLS
CHUNKS = ROWS // 2
EARLY = tuple(range(12))
LATE = tuple(range(12, CHUNKS + 2))
F8_SECTIONS = 9
BF_SECTIONS = 2
UNROLL = 3
LAG = 8
PACKET = S_PAD + 8
PAIR = 4
ORDER_SCALE = 8.0
STOICH_SCALE = 64.0
RATE_SCALE = 32.0

bf16 = jnp.bfloat16
f8 = jnp.float8_e4m3fn
f32 = jnp.float32
MESH = pl.DeviceIdType.MESH


def step_table():
    table = np.zeros((16, MOST), np.float32)
    for count in range(1, MOST + 1):
        for j in range(count):
            node = np.cos(np.pi * (2 * j + 1) / (2 * count))
            table[count, MOST - count + j] = 1.0 / (4.5 + 3.5 * node)
    return table


def split(value, dtype):
    high = value.astype(dtype)
    return high, (value - high.astype(f32)).astype(dtype)


def dot(left, right):
    return jnp.dot(left, right, preferred_element_type=f32)


def block(b):
    return pl.ds(b * CELLS, CELLS)


def blocks_of(c):
    return tuple(b for b in (2 * c, 2 * c + 1) if b < ROWS + HALO)


def chunk(c):
    return pl.ds(c * 2 * CELLS, len(blocks_of(c)) * CELLS)


def kernel(
    sec_hbm, tab_hbm, steps_hbm, comp_hbm, theta_hbm, orders_hbm, stoich_hbm, prefactor_hbm,
    activation_hbm, diff_hbm, out, sec, tab, counts, steps, comp, theta, orders, stoich,
    log_prefactor, activation, diffusivity, vs, base, rate, rate_b, f_b, f_8, orders_8, orders_b,
    stoich_8, stoich_b, prefactor_col, activation_col, diff_col, packets, halo, halo_start,
    halo_steps, load_sems, send_sems, recv_sems,
):
    gx, gy = lax.axis_index("gx"), lax.axis_index("gy")
    nx, ny = lax.axis_size("gx"), lax.axis_size("gy")
    sides = (
        (gx > 0, (gx - 1, gy)),
        (gx < nx - 1, (gx + 1, gy)),
        (gy > 0, (gx, gy - 1)),
        (gy < ny - 1, (gx, gy + 1)),
    )
    peers = (gx + nx - 1) // nx + (2 * nx - 2 - gx) // nx
    peers = peers + (gy + ny - 1) // ny + (2 * ny - 2 - gy) // ny
    next_to_first = 1 - (gx + gy + nx + ny - 2) // (nx + ny) - (1 - (gx + gy + nx + ny - 1) // (nx + ny))
    far = 1 - (gx % 4 + 3) // 4
    far = jnp.maximum(far * ((gx + nx - 1) // nx), (gy % 16) // 15 * ((2 * ny - 2 - gy) // ny))
    turn = far + (2 - far) * next_to_first

    pairs = (
        (comp_hbm, comp),
        (theta_hbm, theta),
        (sec_hbm, sec),
        (sec_hbm, counts),
        (prefactor_hbm, log_prefactor),
        (activation_hbm, activation),
        (stoich_hbm, stoich),
        (orders_hbm, orders),
        (diff_hbm, diffusivity),
        (tab_hbm, tab),
        (steps_hbm, steps),
    )
    loads = [pltpu.make_async_copy(a, b, load_sems.at[i]) for i, (a, b) in enumerate(pairs)]
    for load in loads:
        load.start()
    barrier = pltpu.get_barrier_semaphore()
    for there, device in sides:

        @pl.when(there)
        def _(device=device):
            pl.semaphore_signal(barrier, inc=1, device_id=device, device_id_type=MESH)

    for k, (there, _) in enumerate(sides):

        @pl.when(jnp.logical_not(there))
        def _(k=k):
            halo[k] = jnp.zeros((PACKET, CELLS), f32)

    copies = [
        pltpu.make_async_remote_copy(
            src_ref=packets.at[min(k, 2)],
            dst_ref=halo.at[k ^ 1],
            send_sem=send_sems.at[k],
            recv_sem=recv_sems.at[k],
            device_id=sides[k][1],
            device_id_type=MESH,
        )
        for k in range(4)
    ]

    def send_at(point):
        @pl.when(turn == point)
        def _():
            pl.semaphore_wait(barrier, peers)
            for k, (there, _) in enumerate(sides):

                @pl.when(there)
                def _(k=k):
                    copies[k].start()

    for load in loads[1:]:
        load.wait()
    orders_f = jnp.concatenate([orders[...] * 0.5, jnp.zeros((V_PAD - SPECIES, REACTIONS), f32)], 0)
    orders_f = jnp.concatenate([orders_f, jnp.zeros((V_PAD, 384 - REACTIONS), f32)], 1)
    orders_f = jnp.transpose(orders_f)[:R_PAD]
    high, low = split(orders_f, bf16)
    orders_b[...] = jnp.concatenate([high, high, low], 1)
    high, low = split(orders_f * ORDER_SCALE, f8)
    orders_8[...] = jnp.concatenate([high, high, low, low], 1)
    stoich_f = jnp.concatenate([stoich[...] * 0.5, jnp.zeros((V_PAD - SPECIES, REACTIONS), f32)], 0)
    stoich_f = jnp.concatenate([stoich_f, jnp.zeros((V_PAD, R_PAD - REACTIONS), f32)], 1)
    high, low = split(stoich_f * (1.0 / RATE_SCALE), bf16)
    stoich_b[...] = jnp.concatenate([high, low], 0)
    stoich_8[...] = (stoich_f * STOICH_SCALE).astype(f8)
    rows = [log_prefactor[...].reshape(1, REACTIONS), activation[...].reshape(1, REACTIONS)]
    rows = jnp.concatenate(rows + [jnp.zeros((6, REACTIONS), f32)], 0)
    rows = jnp.concatenate([rows, jnp.zeros((8, 384 - REACTIONS), f32)], 1)
    columns = jnp.transpose(rows)
    prefactor_col[...] = jnp.broadcast_to(columns[:R_PAD, 0:1], (R_PAD, CELLS))
    activation_col[...] = jnp.broadcast_to(columns[:R_PAD, 1:2], (R_PAD, CELLS))
    rows = jnp.concatenate([diffusivity[...], jnp.zeros((1, CELLS - SPECIES), f32)], 1)
    rows = jnp.concatenate([rows, jnp.zeros((7, CELLS), f32)], 0)
    diff_col[...] = jnp.broadcast_to(jnp.transpose(rows)[:S_PAD, 0:1], (S_PAD, CELLS))

    lane = lax.broadcasted_iota(jnp.int32, (S_PAD, CELLS), 1)
    rest = jnp.zeros((6, CELLS), f32)
    loads[0].wait()

    def start_of(b):
        if b >= ROWS:
            return halo_start[:, block(b - ROWS)]
        value = comp[pl.ds(b, SPECIES, stride=ROWS), :]
        return jnp.concatenate([value, jnp.zeros((S_PAD - SPECIES, CELLS), f32)], 0)

    vs[S_PAD:, :] = jnp.zeros((V_PAD - S_PAD, WIDE), f32)
    packed = jnp.zeros((S_PAD, CELLS), f32)
    for b in range(ROWS):
        v = start_of(b)
        vs[0:S_PAD, block(b)] = v
        packed = jnp.where(lane == b, pltpu.roll(v, b, 1), packed)
        packed = jnp.where(lane == 64 + b, pltpu.roll(v, (64 + b + 1) % CELLS, 1), packed)
        if b in (0, ROWS - 1):
            count = jnp.full((1, CELLS), sec[0, b].astype(f32))
            tail = jnp.concatenate([theta[b : b + 1, :], count, rest], 0)
            packets[b // (ROWS - 1)] = jnp.concatenate([v, tail], 0)
    temps = jnp.concatenate([theta[...], jnp.zeros((CELLS - ROWS, CELLS), f32)], 0)
    temps = jnp.transpose(temps)
    temps = temps[0:1, :] + pltpu.roll(temps[CELLS - 8 : CELLS, :], 64, 1)[7:8, :]
    count = jnp.concatenate([counts[...].astype(f32), jnp.zeros((1, CELLS - ROWS), f32)], 1)
    count = jnp.broadcast_to(count, (8, CELLS))
    count = (count + pltpu.roll(count, 64, 1))[0:1, :]
    packets[2] = jnp.concatenate([packed, temps, count, rest], 0)

    send_at(0)

    def set_rate(b, temp):
        r = jnp.exp(prefactor_col[...] - activation_col[...] * temp) * RATE_SCALE
        rate[:, block(b)] = r
        rate_b[:, block(b)] = r.astype(bf16)

    def set_base(c):
        bias = dot(stoich_b[0:S_PAD, :], rate_b[:, chunk(c)])
        base[:, chunk(c)] = vs[0:S_PAD, chunk(c)] + bias

    for c in range(CHUNKS):
        for b in blocks_of(c):
            set_rate(b, theta[b : b + 1, :])
        set_base(c)

    def forward_f8(c):
        high, low = split(vs[:, chunk(c)] * (1.0 / ORDER_SCALE), f8)
        drive = dot(orders_8[...], jnp.concatenate([high, low, high, low], 0))
        f_8[:, chunk(c)] = (jnp.tanh(drive.astype(bf16)) * rate_b[:, chunk(c)]).astype(f8)

    def forward_bf(c):
        drive = dot(orders_b[:, 0:V_PAD], vs[:, chunk(c)].astype(bf16))
        f_b[:, chunk(c)] = (jnp.tanh(drive) * rate[:, chunk(c)]).astype(bf16)

    def update(c, j, target):
        for h, b in enumerate(blocks_of(c)):
            if b < ROWS:
                step = tab[sec[0, b], j]
            else:
                step = halo_steps[j, :, block(b - ROWS)][0:1]
            v = vs[0:S_PAD, block(b)]
            vs[0:S_PAD, block(b)] = v + step * (target[:, h * CELLS : (h + 1) * CELLS] - v)

    def relax_f8(c, j):
        product = dot(stoich_8[...], f_8[:, chunk(c)])[0:S_PAD]
        update(c, j, base[:, chunk(c)] + product * (1.0 / (STOICH_SCALE * RATE_SCALE)))

    def relax_bf(c, j):
        update(c, j, base[:, chunk(c)] + dot(stoich_b[0:S_PAD, :], f_b[:, chunk(c)]))

    def section(chunks, j, forward, relax):
        for first in range(0, len(chunks) + LAG, PAIR):
            for at in range(first, first + PAIR):
                if at < len(chunks):
                    forward(chunks[at])
            for at in range(first, first + PAIR):
                if LAG <= at < len(chunks) + LAG:
                    relax(chunks[at - LAG], j)

    def sections_f8(chunks):
        def some(i, _):
            for u in range(UNROLL):
                section(chunks, i * UNROLL + u, forward_f8, relax_f8)
            return 0

        lax.fori_loop(0, F8_SECTIONS // UNROLL, some, 0)

    def sections_bf(chunks):
        for j in range(F8_SECTIONS, F8_SECTIONS + BF_SECTIONS):
            section(chunks, j, forward_bf, relax_bf)

    def last_section(c):
        high, low = split(vs[:, chunk(c)], bf16)
        drive = dot(orders_b[...], jnp.concatenate([high, low, high], 0))
        r = rate[:, chunk(c)]
        high, low = split(r + r * jnp.tanh(drive), bf16)
        product = dot(stoich_b[...], high)
        source = product[0:S_PAD] + product[V_PAD : V_PAD + S_PAD] + dot(stoich_b[0:S_PAD, :], low)
        start = [start_of(b) for b in blocks_of(c)]
        start = jnp.concatenate(start, 1) if len(start) > 1 else start[0]
        update(c, MOST - 1, start + source)

    sections_f8(EARLY)
    send_at(1)
    sections_bf(EARLY)
    for c in EARLY:
        last_section(c)
    send_at(2)

    for k, (there, _) in enumerate(sides):

        @pl.when(there)
        def _(k=k):
            copies[k ^ 1].wait_recv()

    side = lax.broadcasted_iota(jnp.int32, (PACKET, CELLS), 1) < 64
    which = lax.broadcasted_iota(jnp.int32, (16, CELLS), 0).astype(f32)
    for q in range(HALO):
        packet = halo[q] if q < 2 else jnp.where(side, halo[3], halo[2])
        halo_start[:, block(q)] = packet[0:S_PAD]
        vs[0:S_PAD, block(ROWS + q)] = packet[0:S_PAD]
        count = jnp.broadcast_to(packet[S_PAD + 1 : S_PAD + 2], (16, CELLS))
        found = jnp.dot(
            steps[...],
            jnp.where(count == which, 1.0, 0.0),
            precision=lax.Precision.HIGHEST,
            preferred_element_type=f32,
        )
        for j in range(MOST):
            halo_steps[j, :, block(q)] = jnp.broadcast_to(found[j : j + 1], (8, CELLS))
        set_rate(ROWS + q, packet[S_PAD : S_PAD + 1])
    for c in range(CHUNKS, CHUNKS + 2):
        set_base(c)

    sections_f8(LATE)
    sections_bf(LATE)
    for c in LATE:
        last_section(c)

    d = diff_col[...]
    columns = vs[0:S_PAD, block(ROWS + 2)]
    for b in range(ROWS):
        v = vs[0:S_PAD, block(b)]
        above = vs[0:S_PAD, block(b - 1 if b > 0 else ROWS)]
        below = vs[0:S_PAD, block(b + 1 if b < ROWS - 1 else ROWS + 1)]
        before = pltpu.roll(columns, (CELLS - 64 - b) % CELLS, 1)
        before = jnp.where(lane == 0, before, pltpu.roll(v, 1, 1))
        after = pltpu.roll(columns, CELLS - 1 - b, 1)
        after = jnp.where(lane == CELLS - 1, after, pltpu.roll(v, CELLS - 1, 1))
        result = v + d * (above + below + before + after - 4.0 * v)
        out[pl.ds(b, SPECIES, stride=ROWS), :] = result[0:SPECIES]

    for k, (there, _) in enumerate(sides):

        @pl.when(there)
        def _(k=k):
            copies[k].wait_send()


def body(
    composition,
    inverse_temp,
    sections,
    reactant_orders,
    net_stoich,
    log_prefactor,
    activation,
    diffusivity,
):
    scratch = pltpu.VMEM
    operands = (
        sections.reshape(1, ROWS),
        jnp.asarray(step_table()),
        jnp.asarray(np.pad(step_table().T, ((0, 4), (0, 0)))),
        composition.reshape(SPECIES * ROWS, CELLS),
        inverse_temp,
        reactant_orders.T,
        net_stoich,
        log_prefactor,
        activation,
        diffusivity.reshape(1, SPECIES),
    )
    operands = [pltpu.with_memory_space_constraint(x, pltpu.HBM) for x in operands]
    result = pl.pallas_call(
        kernel,
        out_shape=scratch((SPECIES * ROWS, CELLS), f32),
        in_specs=[pl.BlockSpec(memory_space=pltpu.HBM)] * 10,
        out_specs=pl.BlockSpec(memory_space=pltpu.VMEM),
        scratch_shapes=[
            pltpu.SMEM((1, ROWS), jnp.int32),
            pltpu.SMEM((16, MOST), f32),
            scratch((1, ROWS), jnp.int32),
            scratch((16, 16), f32),
            scratch((SPECIES * ROWS, CELLS), f32),
            scratch((ROWS, CELLS), f32),
            scratch((SPECIES, REACTIONS), f32),
            scratch((SPECIES, REACTIONS), f32),
            scratch((REACTIONS,), f32),
            scratch((REACTIONS,), f32),
            scratch((1, SPECIES), f32),
            scratch((V_PAD, WIDE), f32),
            scratch((S_PAD, WIDE), f32),
            scratch((R_PAD, WIDE), f32),
            scratch((R_PAD, WIDE), bf16),
            scratch((R_PAD, WIDE), bf16),
            scratch((R_PAD, WIDE), f8),
            scratch((R_PAD, 4 * V_PAD), f8),
            scratch((R_PAD, 3 * V_PAD), bf16),
            scratch((V_PAD, R_PAD), f8),
            scratch((2 * V_PAD, R_PAD), bf16),
            scratch((R_PAD, CELLS), f32),
            scratch((R_PAD, CELLS), f32),
            scratch((S_PAD, CELLS), f32),
            scratch((3, PACKET, CELLS), f32),
            scratch((4, PACKET, CELLS), f32),
            scratch((S_PAD, HALO * CELLS), f32),
            scratch((MOST, 8, HALO * CELLS), f32),
            pltpu.SemaphoreType.DMA((11,)),
            pltpu.SemaphoreType.DMA((4,)),
            pltpu.SemaphoreType.DMA((4,)),
        ],
        compiler_params=pltpu.CompilerParams(
            collective_id=0, has_side_effects=True, vmem_limit_bytes=48 << 20
        ),
    )(*operands)
    return result.reshape(SPECIES, ROWS, CELLS)


def solution(mesh):
    return jax.shard_map(
        body,
        mesh=mesh,
        in_specs=(P(None, "gx", "gy"), P("gx", "gy"), P("gx", "gy"), P(), P(), P(), P(), P()),
        out_specs=P(None, "gx", "gy"),
        check_vma=False,
    )
```

```python
import functools

import jax
import jax.numpy as jnp
import numpy as np
from jax import lax
from jax.experimental import pallas as pl
from jax.experimental.pallas import tpu as pltpu
from jax.sharding import PartitionSpec as P

SPECIES = 53
REACTIONS = 325
ROWS = 32
CELLS = 128
MOST = 12
S_PAD = 56
V_PAD = 64
R_PAD = 352
HALO = 3
WIDE = (ROWS + HALO) * CELLS
CHUNKS = ROWS // 2
EARLY = tuple(range(12))
LATE = tuple(range(12, CHUNKS + 2))
F8_SECTIONS = 9
BF_SECTIONS = 2
UNROLL = 3
LAG = 4
PACKET = S_PAD + 8
PAIR = 4
ORDER_SCALE = 8.0
STOICH_SCALE = 64.0
RATE_SCALE = 32.0

bf16 = jnp.bfloat16
f8 = jnp.float8_e4m3fn
f32 = jnp.float32
MESH = pl.DeviceIdType.MESH


def step_table():
    table = np.zeros((16, MOST), np.float32)
    for count in range(1, MOST + 1):
        for j in range(count):
            node = np.cos(np.pi * (2 * j + 1) / (2 * count))
            table[count, MOST - count + j] = 1.0 / (4.5 + 3.5 * node)
    return table


def split(value, dtype):
    high = value.astype(dtype)
    return high, (value - high.astype(f32)).astype(dtype)


def dot(left, right):
    return jnp.dot(left, right, preferred_element_type=f32)


def block(b):
    return pl.ds(b * CELLS, CELLS)


def blocks_of(c):
    return tuple(b for b in (2 * c, 2 * c + 1) if b < ROWS + HALO)


def chunk(c):
    return pl.ds(c * 2 * CELLS, len(blocks_of(c)) * CELLS)


def kernel(
    sec_hbm, tab_hbm, steps_hbm, comp_hbm, theta_hbm, orders_hbm, stoich_hbm, prefactor_hbm,
    activation_hbm, diff_hbm, out, sec, tab, counts, steps, comp, theta, orders, stoich,
    log_prefactor, activation, diffusivity, vs, base, rate, rate_b, f_b, f_8, orders_8, orders_b,
    stoich_8, stoich_b, prefactor_col, activation_col, diff_col, packets, halo, halo_start,
    halo_steps, load_sems, send_sems, recv_sems,
):
    gx, gy = lax.axis_index("gx"), lax.axis_index("gy")
    nx, ny = lax.axis_size("gx"), lax.axis_size("gy")
    sides = (
        (gx > 0, (gx - 1, gy)),
        (gx < nx - 1, (gx + 1, gy)),
        (gy > 0, (gx, gy - 1)),
        (gy < ny - 1, (gx, gy + 1)),
    )
    peers = (gx + nx - 1) // nx + (2 * nx - 2 - gx) // nx
    peers = peers + (gy + ny - 1) // ny + (2 * ny - 2 - gy) // ny
    next_to_first = 1 - (gx + gy + nx + ny - 2) // (nx + ny)
    next_to_first = next_to_first - (1 - (gx + gy + nx + ny - 1) // (nx + ny))
    inner, upper = gx % 4, gy // 16
    row_far = (1 - (inner + 3) // 4) * ((gx + nx - 1) // nx) * (2 - jnp.minimum(upper, 1))
    column_far = (gy % 16) // 15 * ((2 * ny - 2 - gy) // ny) * (2 - inner // 2)
    turn = jnp.maximum(jnp.maximum(row_far, column_far), 3 * next_to_first)

    pairs = (
        (comp_hbm, comp),
        (theta_hbm, theta),
        (sec_hbm, sec),
        (sec_hbm, counts),
        (prefactor_hbm, log_prefactor),
        (activation_hbm, activation),
        (stoich_hbm, stoich),
        (orders_hbm, orders),
        (diff_hbm, diffusivity),
        (tab_hbm, tab),
        (steps_hbm, steps),
    )
    loads = [pltpu.make_async_copy(a, b, load_sems.at[i]) for i, (a, b) in enumerate(pairs)]
    for load in loads:
        load.start()
    barrier = pltpu.get_barrier_semaphore()
    for there, device in sides:

        @pl.when(there)
        def _(device=device):
            pl.semaphore_signal(barrier, inc=1, device_id=device, device_id_type=MESH)

    for k, (there, _) in enumerate(sides):

        @pl.when(jnp.logical_not(there))
        def _(k=k):
            halo[k] = jnp.zeros((PACKET, CELLS), f32)

    copies = [
        pltpu.make_async_remote_copy(
            src_ref=packets.at[min(k, 2)],
            dst_ref=halo.at[k ^ 1],
            send_sem=send_sems.at[k],
            recv_sem=recv_sems.at[k],
            device_id=sides[k][1],
            device_id_type=MESH,
        )
        for k in range(4)
    ]

    def send_at(point):
        @pl.when(turn == point)
        def _():
            pl.semaphore_wait(barrier, peers)
            for k, (there, _) in enumerate(sides):

                @pl.when(there)
                def _(k=k):
                    copies[k].start()

    for load in loads[1:]:
        load.wait()
    orders_f = jnp.concatenate([orders[...] * 0.5, jnp.zeros((V_PAD - SPECIES, REACTIONS), f32)], 0)
    orders_f = jnp.concatenate([orders_f, jnp.zeros((V_PAD, 384 - REACTIONS), f32)], 1)
    orders_f = jnp.transpose(orders_f)[:R_PAD]
    high, low = split(orders_f, bf16)
    orders_b[...] = jnp.concatenate([high, high, low], 1)
    orders_8[...] = (orders_f * ORDER_SCALE).astype(f8)
    stoich_f = jnp.concatenate([stoich[...] * 0.5, jnp.zeros((V_PAD - SPECIES, REACTIONS), f32)], 0)
    stoich_f = jnp.concatenate([stoich_f, jnp.zeros((V_PAD, R_PAD - REACTIONS), f32)], 1)
    high, low = split(stoich_f * (1.0 / RATE_SCALE), bf16)
    stoich_b[...] = jnp.concatenate([high, low], 0)
    stoich_8[...] = (stoich_f * STOICH_SCALE).astype(f8)
    rows = [log_prefactor[...].reshape(1, REACTIONS), activation[...].reshape(1, REACTIONS)]
    rows = jnp.concatenate(rows + [jnp.zeros((6, REACTIONS), f32)], 0)
    rows = jnp.concatenate([rows, jnp.zeros((8, 384 - REACTIONS), f32)], 1)
    columns = jnp.transpose(rows)
    prefactor_col[...] = jnp.broadcast_to(columns[:R_PAD, 0:1], (R_PAD, CELLS))
    activation_col[...] = jnp.broadcast_to(columns[:R_PAD, 1:2], (R_PAD, CELLS))
    rows = jnp.concatenate([diffusivity[...], jnp.zeros((1, CELLS - SPECIES), f32)], 1)
    rows = jnp.concatenate([rows, jnp.zeros((7, CELLS), f32)], 0)
    diff_col[...] = jnp.broadcast_to(jnp.transpose(rows)[:S_PAD, 0:1], (S_PAD, CELLS))

    lane = lax.broadcasted_iota(jnp.int32, (S_PAD, CELLS), 1)
    rest = jnp.zeros((6, CELLS), f32)
    loads[0].wait()

    def start_of(b):
        if b >= ROWS:
            return halo_start[:, block(b - ROWS)]
        value = comp[pl.ds(b, SPECIES, stride=ROWS), :]
        return jnp.concatenate([value, jnp.zeros((S_PAD - SPECIES, CELLS), f32)], 0)

    vs[S_PAD:, :] = jnp.zeros((V_PAD - S_PAD, WIDE), f32)
    packed = jnp.zeros((S_PAD, CELLS), f32)
    for b in range(ROWS):
        v = start_of(b)
        vs[0:S_PAD, block(b)] = v
        packed = jnp.where(lane == b, pltpu.roll(v, b, 1), packed)
        packed = jnp.where(lane == 64 + b, pltpu.roll(v, (64 + b + 1) % CELLS, 1), packed)
        if b in (0, ROWS - 1):
            count = jnp.full((1, CELLS), sec[0, b].astype(f32))
            tail = jnp.concatenate([theta[b : b + 1, :], count, rest], 0)
            packets[b // (ROWS - 1)] = jnp.concatenate([v, tail], 0)
    temps = jnp.concatenate([theta[...], jnp.zeros((CELLS - ROWS, CELLS), f32)], 0)
    temps = jnp.transpose(temps)
    temps = temps[0:1, :] + pltpu.roll(temps[CELLS - 8 : CELLS, :], 64, 1)[7:8, :]
    count = jnp.concatenate([counts[...].astype(f32), jnp.zeros((1, CELLS - ROWS), f32)], 1)
    count = jnp.broadcast_to(count, (8, CELLS))
    count = (count + pltpu.roll(count, 64, 1))[0:1, :]
    packets[2] = jnp.concatenate([packed, temps, count, rest], 0)

    send_at(0)

    def set_rate(b, temp):
        r = jnp.exp(prefactor_col[...] - activation_col[...] * temp) * RATE_SCALE
        rate[:, block(b)] = r
        rate_b[:, block(b)] = r.astype(bf16)

    def set_base(c):
        bias = dot(stoich_b[0:S_PAD, :], rate_b[:, chunk(c)])
        base[:, chunk(c)] = vs[0:S_PAD, chunk(c)] + bias

    for c in range(CHUNKS):
        for b in blocks_of(c):
            set_rate(b, theta[b : b + 1, :])
        set_base(c)

    send_at(1)

    def forward_f8(c):
        drive = dot(orders_8[...], (vs[:, chunk(c)] * (1.0 / ORDER_SCALE)).astype(f8))
        f_8[:, chunk(c)] = (jnp.tanh(drive.astype(bf16)) * rate_b[:, chunk(c)]).astype(f8)

    def forward_bf(c):
        drive = dot(orders_b[:, 0:V_PAD], vs[:, chunk(c)].astype(bf16))
        f_b[:, chunk(c)] = (jnp.tanh(drive) * rate[:, chunk(c)]).astype(bf16)

    def update(c, j, target):
        for h, b in enumerate(blocks_of(c)):
            if b < ROWS:
                step = tab[sec[0, b], j]
            else:
                step = halo_steps[j, :, block(b - ROWS)][0:1]
            v = vs[0:S_PAD, block(b)]
            vs[0:S_PAD, block(b)] = v + step * (target[:, h * CELLS : (h + 1) * CELLS] - v)

    def relax_f8(c, j):
        product = dot(stoich_8[...], f_8[:, chunk(c)])[0:S_PAD]
        update(c, j, base[:, chunk(c)] + product * (1.0 / (STOICH_SCALE * RATE_SCALE)))

    def relax_bf(c, j):
        update(c, j, base[:, chunk(c)] + dot(stoich_b[0:S_PAD, :], f_b[:, chunk(c)]))

    def section(chunks, j, forward, relax):
        for first in range(0, len(chunks) + LAG, PAIR):
            for at in range(first, first + PAIR):
                if at < len(chunks):
                    forward(chunks[at])
            for at in range(first, first + PAIR):
                if LAG <= at < len(chunks) + LAG:
                    relax(chunks[at - LAG], j)

    def sections_f8(chunks, start, end):
        def some(i, _):
            for u in range(UNROLL):
                section(chunks, i * UNROLL + u, forward_f8, relax_f8)
            return 0

        lax.fori_loop(start // UNROLL, end // UNROLL, some, 0)

    def sections_bf(chunks):
        for j in range(F8_SECTIONS, F8_SECTIONS + BF_SECTIONS):
            section(chunks, j, forward_bf, relax_bf)

    def last_section(c):
        high, low = split(vs[:, chunk(c)], bf16)
        drive = dot(orders_b[...], jnp.concatenate([high, low, high], 0))
        r = rate[:, chunk(c)]
        high, low = split(r + r * jnp.tanh(drive), bf16)
        product = dot(stoich_b[...], high)
        source = product[0:S_PAD] + product[V_PAD : V_PAD + S_PAD] + dot(stoich_b[0:S_PAD, :], low)
        start = [start_of(b) for b in blocks_of(c)]
        start = jnp.concatenate(start, 1) if len(start) > 1 else start[0]
        update(c, MOST - 1, start + source)

    sections_f8(EARLY, 0, 3)
    send_at(2)
    sections_f8(EARLY, 3, F8_SECTIONS)
    sections_bf(EARLY)
    for c in EARLY:
        last_section(c)
    send_at(3)

    for k, (there, _) in enumerate(sides):

        @pl.when(there)
        def _(k=k):
            copies[k ^ 1].wait_recv()

    side = lax.broadcasted_iota(jnp.int32, (PACKET, CELLS), 1) < 64
    which = lax.broadcasted_iota(jnp.int32, (16, CELLS), 0).astype(f32)
    for q in range(HALO):
        packet = halo[q] if q < 2 else jnp.where(side, halo[3], halo[2])
        halo_start[:, block(q)] = packet[0:S_PAD]
        vs[0:S_PAD, block(ROWS + q)] = packet[0:S_PAD]
        count = jnp.broadcast_to(packet[S_PAD + 1 : S_PAD + 2], (16, CELLS))
        found = jnp.dot(
            steps[...],
            jnp.where(count == which, 1.0, 0.0),
            precision=lax.Precision.HIGHEST,
            preferred_element_type=f32,
        )
        for j in range(MOST):
            halo_steps[j, :, block(q)] = jnp.broadcast_to(found[j : j + 1], (8, CELLS))
        set_rate(ROWS + q, packet[S_PAD : S_PAD + 1])
    for c in range(CHUNKS, CHUNKS + 2):
        set_base(c)

    sections_f8(LATE, 0, F8_SECTIONS)
    sections_bf(LATE)
    for c in LATE:
        last_section(c)

    d = diff_col[...]
    columns = vs[0:S_PAD, block(ROWS + 2)]
    for b in range(ROWS):
        v = vs[0:S_PAD, block(b)]
        above = vs[0:S_PAD, block(b - 1 if b > 0 else ROWS)]
        below = vs[0:S_PAD, block(b + 1 if b < ROWS - 1 else ROWS + 1)]
        before = pltpu.roll(columns, (CELLS - 64 - b) % CELLS, 1)
        before = jnp.where(lane == 0, before, pltpu.roll(v, 1, 1))
        after = pltpu.roll(columns, CELLS - 1 - b, 1)
        after = jnp.where(lane == CELLS - 1, after, pltpu.roll(v, CELLS - 1, 1))
        result = v + d * (above + below + before + after - 4.0 * v)
        out[pl.ds(b, SPECIES, stride=ROWS), :] = result[0:SPECIES]

    for k, (there, _) in enumerate(sides):

        @pl.when(there)
        def _(k=k):
            copies[k].wait_send()


def body(
    composition,
    inverse_temp,
    sections,
    reactant_orders,
    net_stoich,
    log_prefactor,
    activation,
    diffusivity,
):
    scratch = pltpu.VMEM
    operands = (
        sections.reshape(1, ROWS),
        jnp.asarray(step_table()),
        jnp.asarray(np.pad(step_table().T, ((0, 4), (0, 0)))),
        composition.reshape(SPECIES * ROWS, CELLS),
        inverse_temp,
        reactant_orders.T,
        net_stoich,
        log_prefactor,
        activation,
        diffusivity.reshape(1, SPECIES),
    )
    operands = [pltpu.with_memory_space_constraint(x, pltpu.HBM) for x in operands]
    result = pl.pallas_call(
        kernel,
        out_shape=scratch((SPECIES * ROWS, CELLS), f32),
        in_specs=[pl.BlockSpec(memory_space=pltpu.HBM)] * 10,
        out_specs=pl.BlockSpec(memory_space=pltpu.VMEM),
        scratch_shapes=[
            pltpu.SMEM((1, ROWS), jnp.int32),
            pltpu.SMEM((16, MOST), f32),
            scratch((1, ROWS), jnp.int32),
            scratch((16, 16), f32),
            scratch((SPECIES * ROWS, CELLS), f32),
            scratch((ROWS, CELLS), f32),
            scratch((SPECIES, REACTIONS), f32),
            scratch((SPECIES, REACTIONS), f32),
            scratch((REACTIONS,), f32),
            scratch((REACTIONS,), f32),
            scratch((1, SPECIES), f32),
            scratch((V_PAD, WIDE), f32),
            scratch((S_PAD, WIDE), f32),
            scratch((R_PAD, WIDE), f32),
            scratch((R_PAD, WIDE), bf16),
            scratch((R_PAD, WIDE), bf16),
            scratch((R_PAD, WIDE), f8),
            scratch((R_PAD, V_PAD), f8),
            scratch((R_PAD, 3 * V_PAD), bf16),
            scratch((V_PAD, R_PAD), f8),
            scratch((2 * V_PAD, R_PAD), bf16),
            scratch((R_PAD, CELLS), f32),
            scratch((R_PAD, CELLS), f32),
            scratch((S_PAD, CELLS), f32),
            scratch((3, PACKET, CELLS), f32),
            scratch((4, PACKET, CELLS), f32),
            scratch((S_PAD, HALO * CELLS), f32),
            scratch((MOST, 8, HALO * CELLS), f32),
            pltpu.SemaphoreType.DMA((11,)),
            pltpu.SemaphoreType.DMA((4,)),
            pltpu.SemaphoreType.DMA((4,)),
        ],
        compiler_params=pltpu.CompilerParams(
            collective_id=0, has_side_effects=True, vmem_limit_bytes=48 << 20
        ),
    )(*operands)
    return result.reshape(SPECIES, ROWS, CELLS)


def solution(mesh):
    return jax.shard_map(
        body,
        mesh=mesh,
        in_specs=(P(None, "gx", "gy"), P("gx", "gy"), P("gx", "gy"), P(), P(), P(), P(), P()),
        out_specs=P(None, "gx", "gy"),
        check_vma=False,
    )
```

```python
import functools

import jax
import jax.numpy as jnp
import numpy as np
from jax import lax
from jax.experimental import pallas as pl
from jax.experimental.pallas import tpu as pltpu
from jax.sharding import PartitionSpec as P

SPECIES = 53
REACTIONS = 325
ROWS = 32
CELLS = 128
MOST = 12
S_PAD = 56
V_PAD = 64
R_PAD = 352
HALO = 3
WIDE = (ROWS + HALO) * CELLS
CHUNKS = ROWS // 2
EARLY = tuple(range(12))
LATE = tuple(range(12, CHUNKS + 2))
F8_SECTIONS = 9
BF_SECTIONS = 2
UNROLL = 3
LAG = 4
PACKET = S_PAD + 8
PAIR = 4
ORDER_SCALE = 8.0
STOICH_SCALE = 64.0
RATE_SCALE = 32.0

bf16 = jnp.bfloat16
f8 = jnp.float8_e4m3fn
f32 = jnp.float32
MESH = pl.DeviceIdType.MESH


def step_table():
    table = np.zeros((16, MOST), np.float32)
    for count in range(1, MOST + 1):
        for j in range(count):
            node = np.cos(np.pi * (2 * j + 1) / (2 * count))
            table[count, MOST - count + j] = 1.0 / (4.5 + 3.5 * node)
    return table


def split(value, dtype):
    high = value.astype(dtype)
    return high, (value - high.astype(f32)).astype(dtype)


def dot(left, right):
    return jnp.dot(left, right, preferred_element_type=f32)


def block(b):
    return pl.ds(b * CELLS, CELLS)


def blocks_of(c):
    return tuple(b for b in (2 * c, 2 * c + 1) if b < ROWS + HALO)


def chunk(c):
    return pl.ds(c * 2 * CELLS, len(blocks_of(c)) * CELLS)


def kernel(
    sec_hbm, tab_hbm, steps_hbm, comp_hbm, theta_hbm, orders_hbm, stoich_hbm, prefactor_hbm,
    activation_hbm, diff_hbm, out, sec, tab, counts, steps, comp, theta, orders, stoich,
    log_prefactor, activation, diffusivity, vs, base, rate, rate_b, f_b, f_8, orders_8, orders_b,
    stoich_8, stoich_b, prefactor_col, activation_col, diff_col, packets, halo, halo_start,
    halo_steps, load_sems, send_sems, recv_sems,
):
    gx, gy = lax.axis_index("gx"), lax.axis_index("gy")
    nx, ny = lax.axis_size("gx"), lax.axis_size("gy")
    sides = (
        (gx > 0, (gx - 1, gy)),
        (gx < nx - 1, (gx + 1, gy)),
        (gy > 0, (gx, gy - 1)),
        (gy < ny - 1, (gx, gy + 1)),
    )
    peers = (gx + nx - 1) // nx + (2 * nx - 2 - gx) // nx
    peers = peers + (gy + ny - 1) // ny + (2 * ny - 2 - gy) // ny
    next_to_first = 1 - (gx + gy + nx + ny - 2) // (nx + ny)
    next_to_first = next_to_first - (1 - (gx + gy + nx + ny - 1) // (nx + ny))
    inner, upper = gx % 4, gy // 16
    row_far = (1 - (inner + 3) // 4) * ((gx + nx - 1) // nx) * (2 - jnp.minimum(upper, 1))
    column_far = (gy % 16) // 15 * ((2 * ny - 2 - gy) // ny) * 2
    turn = jnp.maximum(jnp.maximum(row_far, column_far), 3 * next_to_first)

    pairs = (
        (comp_hbm, comp),
        (theta_hbm, theta),
        (sec_hbm, sec),
        (sec_hbm, counts),
        (prefactor_hbm, log_prefactor),
        (activation_hbm, activation),
        (stoich_hbm, stoich),
        (orders_hbm, orders),
        (diff_hbm, diffusivity),
        (tab_hbm, tab),
        (steps_hbm, steps),
    )
    loads = [pltpu.make_async_copy(a, b, load_sems.at[i]) for i, (a, b) in enumerate(pairs)]
    for load in loads:
        load.start()
    barrier = pltpu.get_barrier_semaphore()
    for there, device in sides:

        @pl.when(there)
        def _(device=device):
            pl.semaphore_signal(barrier, inc=1, device_id=device, device_id_type=MESH)

    for k, (there, _) in enumerate(sides):

        @pl.when(jnp.logical_not(there))
        def _(k=k):
            halo[k] = jnp.zeros((PACKET, CELLS), f32)

    copies = [
        pltpu.make_async_remote_copy(
            src_ref=packets.at[min(k, 2)],
            dst_ref=halo.at[k ^ 1],
            send_sem=send_sems.at[k],
            recv_sem=recv_sems.at[k],
            device_id=sides[k][1],
            device_id_type=MESH,
        )
        for k in range(4)
    ]

    def send_at(point):
        @pl.when(turn == point)
        def _():
            pl.semaphore_wait(barrier, peers)
            for k, (there, _) in enumerate(sides):

                @pl.when(there)
                def _(k=k):
                    copies[k].start()

    for load in loads[1:]:
        load.wait()
    orders_f = jnp.concatenate([orders[...] * 0.5, jnp.zeros((V_PAD - SPECIES, REACTIONS), f32)], 0)
    orders_f = jnp.concatenate([orders_f, jnp.zeros((V_PAD, 384 - REACTIONS), f32)], 1)
    orders_f = jnp.transpose(orders_f)[:R_PAD]
    high, low = split(orders_f, bf16)
    orders_b[...] = jnp.concatenate([high, high, low], 1)
    orders_8[...] = (orders_f * ORDER_SCALE).astype(f8)
    stoich_f = jnp.concatenate([stoich[...] * 0.5, jnp.zeros((V_PAD - SPECIES, REACTIONS), f32)], 0)
    stoich_f = jnp.concatenate([stoich_f, jnp.zeros((V_PAD, R_PAD - REACTIONS), f32)], 1)
    high, low = split(stoich_f * (1.0 / RATE_SCALE), bf16)
    stoich_b[...] = jnp.concatenate([high, low], 0)
    stoich_8[...] = (stoich_f * STOICH_SCALE).astype(f8)
    rows = [log_prefactor[...].reshape(1, REACTIONS), activation[...].reshape(1, REACTIONS)]
    rows = jnp.concatenate(rows + [jnp.zeros((6, REACTIONS), f32)], 0)
    rows = jnp.concatenate([rows, jnp.zeros((8, 384 - REACTIONS), f32)], 1)
    columns = jnp.transpose(rows)
    prefactor_col[...] = jnp.broadcast_to(columns[:R_PAD, 0:1], (R_PAD, CELLS))
    activation_col[...] = jnp.broadcast_to(columns[:R_PAD, 1:2], (R_PAD, CELLS))
    rows = jnp.concatenate([diffusivity[...], jnp.zeros((1, CELLS - SPECIES), f32)], 1)
    rows = jnp.concatenate([rows, jnp.zeros((7, CELLS), f32)], 0)
    diff_col[...] = jnp.broadcast_to(jnp.transpose(rows)[:S_PAD, 0:1], (S_PAD, CELLS))

    lane = lax.broadcasted_iota(jnp.int32, (S_PAD, CELLS), 1)
    rest = jnp.zeros((6, CELLS), f32)
    loads[0].wait()

    def start_of(b):
        if b >= ROWS:
            return halo_start[:, block(b - ROWS)]
        value = comp[pl.ds(b, SPECIES, stride=ROWS), :]
        return jnp.concatenate([value, jnp.zeros((S_PAD - SPECIES, CELLS), f32)], 0)

    vs[S_PAD:, :] = jnp.zeros((V_PAD - S_PAD, WIDE), f32)
    packed = jnp.zeros((S_PAD, CELLS), f32)
    for b in range(ROWS):
        v = start_of(b)
        vs[0:S_PAD, block(b)] = v
        packed = jnp.where(lane == b, pltpu.roll(v, b, 1), packed)
        packed = jnp.where(lane == 64 + b, pltpu.roll(v, (64 + b + 1) % CELLS, 1), packed)
        if b in (0, ROWS - 1):
            count = jnp.full((1, CELLS), sec[0, b].astype(f32))
            tail = jnp.concatenate([theta[b : b + 1, :], count, rest], 0)
            packets[b // (ROWS - 1)] = jnp.concatenate([v, tail], 0)
    temps = jnp.concatenate([theta[...], jnp.zeros((CELLS - ROWS, CELLS), f32)], 0)
    temps = jnp.transpose(temps)
    temps = temps[0:1, :] + pltpu.roll(temps[CELLS - 8 : CELLS, :], 64, 1)[7:8, :]
    count = jnp.concatenate([counts[...].astype(f32), jnp.zeros((1, CELLS - ROWS), f32)], 1)
    count = jnp.broadcast_to(count, (8, CELLS))
    count = (count + pltpu.roll(count, 64, 1))[0:1, :]
    packets[2] = jnp.concatenate([packed, temps, count, rest], 0)

    send_at(0)

    def set_rate(b, temp):
        r = jnp.exp(prefactor_col[...] - activation_col[...] * temp) * RATE_SCALE
        rate[:, block(b)] = r
        rate_b[:, block(b)] = r.astype(bf16)

    def set_base(c):
        bias = dot(stoich_b[0:S_PAD, :], rate_b[:, chunk(c)])
        base[:, chunk(c)] = vs[0:S_PAD, chunk(c)] + bias

    for c in range(CHUNKS):
        for b in blocks_of(c):
            set_rate(b, theta[b : b + 1, :])
        set_base(c)

    send_at(1)

    def forward_f8(c):
        drive = dot(orders_8[...], (vs[:, chunk(c)] * (1.0 / ORDER_SCALE)).astype(f8))
        f_8[:, chunk(c)] = (jnp.tanh(drive.astype(bf16)) * rate_b[:, chunk(c)]).astype(f8)

    def forward_bf(c):
        drive = dot(orders_b[:, 0:V_PAD], vs[:, chunk(c)].astype(bf16))
        f_b[:, chunk(c)] = (jnp.tanh(drive) * rate[:, chunk(c)]).astype(bf16)

    def update(c, j, target):
        for h, b in enumerate(blocks_of(c)):
            if b < ROWS:
                step = tab[sec[0, b], j]
            else:
                step = halo_steps[j, :, block(b - ROWS)][0:1]
            v = vs[0:S_PAD, block(b)]
            vs[0:S_PAD, block(b)] = v + step * (target[:, h * CELLS : (h + 1) * CELLS] - v)

    def relax_f8(c, j):
        product = dot(stoich_8[...], f_8[:, chunk(c)])[0:S_PAD]
        update(c, j, base[:, chunk(c)] + product * (1.0 / (STOICH_SCALE * RATE_SCALE)))

    def relax_bf(c, j):
        update(c, j, base[:, chunk(c)] + dot(stoich_b[0:S_PAD, :], f_b[:, chunk(c)]))

    def section(chunks, j, forward, relax):
        for first in range(0, len(chunks) + LAG, PAIR):
            for at in range(first, first + PAIR):
                if at < len(chunks):
                    forward(chunks[at])
            for at in range(first, first + PAIR):
                if LAG <= at < len(chunks) + LAG:
                    relax(chunks[at - LAG], j)

    def sections_f8(chunks):
        def some(i, _):
            for u in range(UNROLL):
                section(chunks, i * UNROLL + u, forward_f8, relax_f8)
            return 0

        lax.fori_loop(0, F8_SECTIONS // UNROLL, some, 0)

    def sections_bf(chunks):
        for j in range(F8_SECTIONS, F8_SECTIONS + BF_SECTIONS):
            section(chunks, j, forward_bf, relax_bf)

    def last_section(c):
        high, low = split(vs[:, chunk(c)], bf16)
        drive = dot(orders_b[...], jnp.concatenate([high, low, high], 0))
        r = rate[:, chunk(c)]
        high, low = split(r + r * jnp.tanh(drive), bf16)
        product = dot(stoich_b[...], high)
        source = product[0:S_PAD] + product[V_PAD : V_PAD + S_PAD] + dot(stoich_b[0:S_PAD, :], low)
        start = [start_of(b) for b in blocks_of(c)]
        start = jnp.concatenate(start, 1) if len(start) > 1 else start[0]
        update(c, MOST - 1, start + source)

    sections_f8(EARLY)
    send_at(2)
    sections_bf(EARLY)
    for c in EARLY:
        last_section(c)
    send_at(3)

    for k, (there, _) in enumerate(sides):

        @pl.when(there)
        def _(k=k):
            copies[k ^ 1].wait_recv()

    side = lax.broadcasted_iota(jnp.int32, (PACKET, CELLS), 1) < 64
    which = lax.broadcasted_iota(jnp.int32, (16, CELLS), 0).astype(f32)
    for q in range(HALO):
        packet = halo[q] if q < 2 else jnp.where(side, halo[3], halo[2])
        halo_start[:, block(q)] = packet[0:S_PAD]
        vs[0:S_PAD, block(ROWS + q)] = packet[0:S_PAD]
        count = jnp.broadcast_to(packet[S_PAD + 1 : S_PAD + 2], (16, CELLS))
        found = jnp.dot(
            steps[...],
            jnp.where(count == which, 1.0, 0.0),
            precision=lax.Precision.HIGHEST,
            preferred_element_type=f32,
        )
        for j in range(MOST):
            halo_steps[j, :, block(q)] = jnp.broadcast_to(found[j : j + 1], (8, CELLS))
        set_rate(ROWS + q, packet[S_PAD : S_PAD + 1])
    for c in range(CHUNKS, CHUNKS + 2):
        set_base(c)

    sections_f8(LATE)
    sections_bf(LATE)
    for c in LATE:
        last_section(c)

    d = diff_col[...]
    columns = vs[0:S_PAD, block(ROWS + 2)]
    for b in range(ROWS):
        v = vs[0:S_PAD, block(b)]
        above = vs[0:S_PAD, block(b - 1 if b > 0 else ROWS)]
        below = vs[0:S_PAD, block(b + 1 if b < ROWS - 1 else ROWS + 1)]
        before = pltpu.roll(columns, (CELLS - 64 - b) % CELLS, 1)
        before = jnp.where(lane == 0, before, pltpu.roll(v, 1, 1))
        after = pltpu.roll(columns, CELLS - 1 - b, 1)
        after = jnp.where(lane == CELLS - 1, after, pltpu.roll(v, CELLS - 1, 1))
        result = v + d * (above + below + before + after - 4.0 * v)
        out[pl.ds(b, SPECIES, stride=ROWS), :] = result[0:SPECIES]

    for k, (there, _) in enumerate(sides):

        @pl.when(there)
        def _(k=k):
            copies[k].wait_send()


def body(
    composition,
    inverse_temp,
    sections,
    reactant_orders,
    net_stoich,
    log_prefactor,
    activation,
    diffusivity,
):
    scratch = pltpu.VMEM
    operands = (
        sections.reshape(1, ROWS),
        jnp.asarray(step_table()),
        jnp.asarray(np.pad(step_table().T, ((0, 4), (0, 0)))),
        composition.reshape(SPECIES * ROWS, CELLS),
        inverse_temp,
        reactant_orders.T,
        net_stoich,
        log_prefactor,
        activation,
        diffusivity.reshape(1, SPECIES),
    )
    operands = [pltpu.with_memory_space_constraint(x, pltpu.HBM) for x in operands]
    result = pl.pallas_call(
        kernel,
        out_shape=scratch((SPECIES * ROWS, CELLS), f32),
        in_specs=[pl.BlockSpec(memory_space=pltpu.HBM)] * 10,
        out_specs=pl.BlockSpec(memory_space=pltpu.VMEM),
        scratch_shapes=[
            pltpu.SMEM((1, ROWS), jnp.int32),
            pltpu.SMEM((16, MOST), f32),
            scratch((1, ROWS), jnp.int32),
            scratch((16, 16), f32),
            scratch((SPECIES * ROWS, CELLS), f32),
            scratch((ROWS, CELLS), f32),
            scratch((SPECIES, REACTIONS), f32),
            scratch((SPECIES, REACTIONS), f32),
            scratch((REACTIONS,), f32),
            scratch((REACTIONS,), f32),
            scratch((1, SPECIES), f32),
            scratch((V_PAD, WIDE), f32),
            scratch((S_PAD, WIDE), f32),
            scratch((R_PAD, WIDE), f32),
            scratch((R_PAD, WIDE), bf16),
            scratch((R_PAD, WIDE), bf16),
            scratch((R_PAD, WIDE), f8),
            scratch((R_PAD, V_PAD), f8),
            scratch((R_PAD, 3 * V_PAD), bf16),
            scratch((V_PAD, R_PAD), f8),
            scratch((2 * V_PAD, R_PAD), bf16),
            scratch((R_PAD, CELLS), f32),
            scratch((R_PAD, CELLS), f32),
            scratch((S_PAD, CELLS), f32),
            scratch((3, PACKET, CELLS), f32),
            scratch((4, PACKET, CELLS), f32),
            scratch((S_PAD, HALO * CELLS), f32),
            scratch((MOST, 8, HALO * CELLS), f32),
            pltpu.SemaphoreType.DMA((11,)),
            pltpu.SemaphoreType.DMA((4,)),
            pltpu.SemaphoreType.DMA((4,)),
        ],
        compiler_params=pltpu.CompilerParams(
            collective_id=0, has_side_effects=True, vmem_limit_bytes=48 << 20
        ),
    )(*operands)
    return result.reshape(SPECIES, ROWS, CELLS)


def solution(mesh):
    return jax.shard_map(
        body,
        mesh=mesh,
        in_specs=(P(None, "gx", "gy"), P("gx", "gy"), P("gx", "gy"), P(), P(), P(), P(), P()),
        out_specs=P(None, "gx", "gy"),
        check_vma=False,
    )
```
